32 devices in a mesh: groups: 2 (over y), sec: 4 (over z), op: 4 (over x, core).
Axes of the slice: x: 2, y: 2, z: 4, core: 2. Of those that a mesh axis runs over, the one named last changes fastest.
Arguments:
- psi: bfloat16 [224, 128, 256], P(('groups', 'sec')), parts along dimension 0, may hold values from -6 to 6
- left_ops: bfloat16 [4, 56, 128, 128], P('op', ('groups', 'sec')), parts along dimension 1, may hold values from -0.25 to 0.25
- right_ops: bfloat16 [4, 56, 256, 256], P('op', ('groups', 'sec')), parts along dimension 1, may hold values from -0.375 to 0.375
- left_dims: int32 [56], P('groups'), parts along dimension 0, may hold values from 32 to 128, as said below
- right_dims: int32 [56], P('groups'), parts along dimension 0, may hold values from 64 to 256, as said below
- block_left: int32 [224], P('groups'), parts along dimension 0, may hold values from 0 to 6
- block_right: int32 [224], P('groups'), parts along dimension 0, may hold values from 0 to 6
- right_owner: int32 [224], P('groups'), parts along dimension 0, may hold values from 0 to 3, as said below
Outputs:
- sigma_first: bfloat16 [224, 128, 256], P(('groups', 'sec'), 'op'), parts along dimension 0
- sigma_second: bfloat16 [224, 128, 256], P(('groups', 'sec'), 'op'), parts along dimension 0
The draws below stay inside these ranges and needn't reach their ends.
There are 2 independent parts, one for each index of `groups`. The reference program is written for one: setup_inputs(seed, part) draws one part's arguments, and reference() takes and returns one part's arrays. A program takes and returns all parts, laid end to end along the dimension named above; each array names one. Nothing has to cross between parts.
Inputs may be any that keep to these rules, and one draw needn't show every extreme that they name: `left_dims`: some left sector has dimension 128. `right_dims`: some right sector has dimension 256. `right_owner`: among the 28 blocks of one left owner (blocks j * 28 to (j + 1) * 28 - 1) no right owner appears more than 7 times, and some appears exactly 7 times.
All inputs are finite; a program needn't handle non-finite values.
Results may differ from the reference program's by a relative error of at most 0.017.
Values may be sent and summed in bfloat16 or wider, within the bound.
A program may use at most 64 MiB of HBM per device.

```python
import jax
import jax.numpy as jnp
from jax import lax

LCAP = 128
RCAP = 256
SL_DEV = 7
SR_DEV = 7
BLK_DEV = 28
TERMS = 4
PCAP = 7
LSECT = 28
RSECT = 28
BLOCKS = 112


def sector_sizes(key, count, largest):
    dims = jax.random.randint(key, (count,), largest // 4, largest + 1)
    picked = jax.random.randint(jax.random.fold_in(key, 7), (), 0, count)
    return dims.at[picked].set(largest).astype(jnp.int32)


def draw_left_dims(key, part):
    key = jax.random.fold_in(key, 1)
    return sector_sizes(key, LSECT, LCAP)


def draw_right_dims(key, part):
    key = jax.random.fold_in(key, 2)
    return sector_sizes(key, RSECT, RCAP)


def draw_right_owner(key, part):
    key = jax.random.fold_in(key, 3)
    owners = BLOCKS // BLK_DEV
    device_keys = jax.random.split(key, owners)

    def single_device(device_key):
        return (jax.random.permutation(device_key, owners * PCAP)[:BLK_DEV] % owners).astype(jnp.int32)
    return jax.vmap(single_device)(device_keys).reshape(BLOCKS)


def plant(array, key, least, high):
    shape = array.shape
    index_at = [jax.random.randint(jax.random.fold_in(key, axis), (), 0, shape[axis]) for axis in range(len(shape))]
    array = array.at[tuple(index_at)].set(least)
    longest = shape.index(max(shape))
    index_at[longest] = (index_at[longest] + 1) % shape[longest]
    return array.at[tuple(index_at)].set(high)


def levels(key, shape, pieces, least, top_value):
    def one(position, parts):
        heights = jax.random.uniform(jax.random.fold_in(jax.random.fold_in(key, 6), position), (parts,), jnp.float32, least / len(pieces), top_value / len(pieces))
        return jnp.repeat(jnp.exp(heights), shape[position] // parts).reshape((-1,) + (1,) * (len(shape) - position - 1))

    factor_of = one(*pieces[0])
    for cut in pieces[1:]:
        factor_of = factor_of * one(*cut)
    return factor_of


def scatter_about(own_key, shape, width, limit, cuts=(), kind=jnp.bfloat16):
    loudness = levels(own_key, shape, cuts, -0.22, 0.18) if cuts else 1.0
    array = jax.random.normal(own_key, shape, jnp.float32) * width * loudness
    return jnp.minimum(jnp.maximum(array, -limit), limit).astype(kind)


def setup_inputs(seed: int = 0, part: int = 0) -> dict:
    splits = jax.random.split(jax.random.key(seed), 9)
    part_keys = jax.random.split(jax.random.fold_in(splits[8], part), 9)
    psi = scatter_about(part_keys[0], (BLOCKS, LCAP, RCAP), 1.0, 6.0, ((0, 4),))
    left_ops = scatter_about(part_keys[1], (TERMS, LSECT, LCAP, LCAP), (LCAP * TERMS) ** -0.5, 0.25, ((0, 4), (1, 4)))
    right_ops = scatter_about(part_keys[2], (TERMS, RSECT, RCAP, RCAP), RCAP ** -0.5, 0.375, ((0, 4), (1, 4)))
    left_dims = draw_left_dims(jax.random.fold_in(jax.random.fold_in(splits[8], part), 71), part)
    right_dims = draw_right_dims(jax.random.fold_in(jax.random.fold_in(splits[8], part), 71), part)
    block_left = plant(jax.random.randint(part_keys[5], (BLOCKS,), 0, SL_DEV), jax.random.fold_in(part_keys[5], 1), 0, SL_DEV - 1).astype(jnp.int32)
    block_right = plant(jax.random.randint(part_keys[6], (BLOCKS,), 0, SR_DEV), jax.random.fold_in(part_keys[6], 1), 0, SR_DEV - 1).astype(jnp.int32)
    right_owner = draw_right_owner(jax.random.fold_in(jax.random.fold_in(splits[8], part), 71), part)
    return dict(psi=psi, left_ops=left_ops, right_ops=right_ops, left_dims=left_dims, right_dims=right_dims, block_left=block_left, block_right=block_right, right_owner=right_owner)


def reference(psi, left_ops, right_ops, left_dims, right_dims, block_left, block_right, right_owner):
    block_count = psi.shape[0]
    sender = jnp.arange(block_count, dtype=jnp.int32) // BLK_DEV
    left_index = (sender * SL_DEV + block_left).astype(jnp.int32)
    right_index = (right_owner * SR_DEV + block_right).astype(jnp.int32)
    row_ids = jnp.arange(LCAP, dtype=jnp.int32)
    col_ids = jnp.arange(RCAP, dtype=jnp.int32)
    live_mask = (row_ids[None, :, None] < left_dims[left_index][:, None, None]) & (col_ids[None, None, :] < right_dims[right_index][:, None, None])
    inputs = jnp.where(live_mask, psi, jnp.zeros_like(psi))

    def left_product(operators, values):
        matrices = operators[left_index].astype(jnp.float32)
        return jnp.einsum("pra,pac->prc", matrices, values.astype(jnp.float32)).astype(jnp.bfloat16)

    def right_product(operators, values):
        matrices = operators[right_index].astype(jnp.float32)
        return jnp.einsum("prc,pdc->prd", values.astype(jnp.float32), matrices).astype(jnp.bfloat16)

    def accumulate(term_fn):
        def add_term(summed, operators):
            return summed + term_fn(operators[0], operators[1]).astype(jnp.float32), None
        summed, unused = lax.scan(add_term, jnp.zeros(psi.shape, jnp.float32), (left_ops, right_ops))
        return summed

    def first_term(left_block, right_block):
        return right_product(right_block, left_product(left_block, inputs))

    sigma_first = jnp.where(live_mask, accumulate(first_term), 0.0).astype(jnp.bfloat16)

    def second_term(left_block, right_block):
        return left_product(left_block, right_product(right_block, sigma_first))

    sigma_second = jnp.where(live_mask, accumulate(second_term), 0.0).astype(jnp.bfloat16)
    return sigma_first, sigma_second
```

```python
import functools

import jax
import jax.numpy as jnp
from jax import lax
from jax.experimental import pallas as pl
from jax.experimental.pallas import tpu as pltpu
from jax.sharding import PartitionSpec as P


def block_masks(row_count, col_count, left_dim, right_dim):
    row_ids = lax.broadcasted_iota(jnp.int32, (1, row_count, 1), 1)
    col_ids = lax.broadcasted_iota(jnp.int32, (1, 1, col_count), 2)
    return (row_ids < left_dim[:, None, None]) & (col_ids < right_dim[:, None, None])


def left_apply(matrices, values):
    return jnp.einsum("pra,pac->prc", matrices, values, preferred_element_type=jnp.float32).astype(
        jnp.bfloat16
    )


def right_apply(matrices, values):
    return jnp.einsum("prc,pdc->prd", values, matrices, preferred_element_type=jnp.float32).astype(
        jnp.bfloat16
    )


def op_combine(terms, live_mask, row_share, op_index):
    own_rows = lax.psum_scatter(
        terms.astype(jnp.bfloat16), "op", scatter_dimension=1, tiled=True
    ).astype(jnp.float32)
    own_mask = lax.dynamic_slice_in_dim(live_mask, op_index * row_share, row_share, 1)
    own_rows = jnp.where(own_mask, own_rows, 0.0).astype(jnp.bfloat16)
    full_sigma = lax.all_gather(own_rows, "op", axis=1, tiled=True)
    return (full_sigma, own_rows)


def body(psi, left_ops, right_ops, left_dims, right_dims, block_left, block_right, right_owner):
    senders = lax.axis_size("sec")
    holders = lax.axis_size("op")
    my_index = lax.axis_index("sec")
    op_index = lax.axis_index("op")
    block_count, left_rows, right_cols = psi.shape
    peer_slots = -(-block_count // senders)
    buffer_len = senders * peer_slots
    left_per = left_ops.shape[1]
    right_per = right_ops.shape[1]
    row_share = left_rows // holders
    owner_table = right_owner.reshape(senders, block_count)
    same_owner = owner_table[:, :, None] == owner_table[:, None, :]
    earlier = lax.broadcasted_iota(jnp.int32, (block_count, block_count), 1) < lax.broadcasted_iota(
        jnp.int32, (block_count, block_count), 0
    )
    order_rank = jnp.sum((same_owner & earlier[None]).astype(jnp.int32), axis=2)
    sender_ids = lax.broadcasted_iota(jnp.int32, (senders, block_count), 0)
    mine_owner = lax.dynamic_index_in_dim(owner_table, my_index, 0, keepdims=False)
    mine_rank = lax.dynamic_index_in_dim(order_rank, my_index, 0, keepdims=False)
    send_pos = mine_owner * peer_slots + mine_rank
    mine_left = lax.dynamic_slice_in_dim(block_left, my_index * block_count, block_count)
    mine_right = lax.dynamic_slice_in_dim(block_right, my_index * block_count, block_count)
    left_mask = block_masks(
        left_rows,
        right_cols,
        left_dims[my_index * left_per + mine_left],
        right_dims[mine_owner * right_per + mine_right],
    )
    slot_ids = jnp.arange(buffer_len, dtype=jnp.int32)
    recv_pos = (sender_ids * peer_slots + order_rank).reshape(-1)
    recv_select = (right_owner == my_index)[None, :] & (recv_pos[None, :] == slot_ids[:, None])
    recv_right = jnp.sum(jnp.where(recv_select, block_right[None, :], 0), axis=1)
    right_matrices = right_ops[0][recv_right]
    left_matrices = left_ops[0][mine_left]
    inputs = jnp.where(left_mask, psi, jnp.zeros_like(psi))
    first_terms = left_apply(left_matrices, inputs)
    operators_back = lax.all_to_all(right_matrices, "sec", split_axis=0, concat_axis=0, tiled=True)
    mine_matrices = jnp.take(operators_back, send_pos, axis=0)
    partial_terms = right_apply(mine_matrices, first_terms)
    full_sigma, sigma_first = op_combine(
        partial_terms.astype(jnp.float32), left_mask, row_share, op_index
    )
    second_terms = left_apply(left_matrices, right_apply(mine_matrices, full_sigma))
    final_rows = lax.psum_scatter(
        second_terms.astype(jnp.float32).astype(jnp.bfloat16), "op", scatter_dimension=1, tiled=True
    ).astype(jnp.float32)
    final_mask = lax.dynamic_slice_in_dim(left_mask, op_index * row_share, row_share, 1)
    sigma_second = jnp.where(final_mask, final_rows, 0.0).astype(jnp.bfloat16)
    return (sigma_first, sigma_second)


MESH = pl.DeviceIdType.MESH
CORES = 2
SKEW = 2
VMEM_BUDGET = 40 * 2**20


def kernel(
    senders,
    holders,
    send_block,
    recv_block,
    send_place,
    left_dims,
    right_dims,
    block_left,
    block_right,
    psi,
    left_ops,
    right_ops,
    out_first,
    out_second,
    packed,
    values,
    partial,
    from_core,
    to_chip,
    from_chip,
    final,
    returned_first,
    returned_second,
    z_send,
    z_recv,
    agx_send,
    agx_recv,
    agc_send,
    agc_recv,
    rsc_send,
    rsc_recv,
    rsx_send,
    rsx_recv,
    *left_recv,
):
    me = lax.axis_index("sec")
    op = lax.axis_index("op")
    chips = holders // CORES
    chip, core = op // CORES, op % CORES
    blocks, rows, cols = psi.shape
    left_per, right_per = left_ops.shape[0], right_ops.shape[0]
    slots = values.shape[2]
    share = rows // holders
    returned = (returned_first, returned_second)

    def share_rows(chip_index, core_index):
        start = (chip_index * CORES + core_index) * share
        return pl.ds(pl.multiple_of(start, share), share)

    own_rows = share_rows(chip, core)
    partner = {"op": chip * CORES + (1 - core)}
    chip_at = [lax.rem(chip + e, chips) for e in range(chips)]
    chip_peer = [{"op": c * CORES + core} for c in chip_at]
    sec_before = [lax.rem(me - d + senders, senders) for d in range(senders)]
    sec_after = [lax.rem(me + d, senders) for d in range(senders)]

    barrier = pltpu.get_barrier_semaphore()
    peers = [{"sec": sec_before[d]} for d in range(1, senders)] + [partner] + chip_peer[1:]
    for peer in peers:
        pl.semaphore_signal(barrier, inc=1, device_id=peer, device_id_type=MESH)

    row_ids = lax.broadcasted_iota(jnp.int32, (share, cols), 0) + op * share
    col_ids = lax.broadcasted_iota(jnp.int32, (share, cols), 1)

    def pack(d):
        def one(k, carry):
            block = send_block[d * slots + k]
            value = psi[block, own_rows, :].astype(jnp.float32)
            gb = me * blocks + block
            row_limit = left_dims[me * left_per + block_left[gb]]
            col_limit = right_dims[sec_before[d] * right_per + block_right[gb]]
            live = (row_ids < row_limit) & (col_ids < col_limit)
            value = jnp.where(live, value, 0.0).astype(jnp.bfloat16)
            if d == 0:
                values[0, 0, k, own_rows, :] = value
            else:
                packed[d, k] = value
            return carry

        lax.fori_loop(0, slots, one, 0, unroll=True)

    def remote(src, dst, send_sem, recv_sem, device):
        copy = pltpu.make_async_remote_copy(
            src_ref=src,
            dst_ref=dst,
            send_sem=send_sem,
            recv_sem=recv_sem,
            device_id=device,
            device_id_type=MESH,
        )
        copy.start()
        sent.append(copy)
        return copy

    sent = []
    inbound, left_in, gather_chip, gather_core, reduce_core, reduce_chip, back = (
        {},
        {},
        {},
        {},
        {},
        {},
        {},
    )

    for d in range(senders):
        pack(d)
    pl.semaphore_wait(barrier, len(peers))
    for d in range(1, senders):
        to = {"sec": sec_before[d]}
        inbound[d] = remote(
            packed.at[d],
            values.at[0, d, :, own_rows, :],
            z_send.at[0, d],
            z_recv.at[0, d],
            to,
        )
        left_in[d] = remote(left_ops, left_recv[d - 1], z_send.at[1, d], z_recv.at[1, d], to)

    def gather_start(t, d):
        if t == 0 and d > 0:
            inbound[d].wait_recv()
        part = values.at[t, d, :, own_rows, :]
        for e in range(1, chips):
            gather_chip[t, d, e] = remote(
                part, part, agx_send.at[t, d, e], agx_recv.at[t, d, e], chip_peer[e]
            )
        gather_core[t, d, 0] = remote(
            part, part, agc_send.at[t, d, 0], agc_recv.at[t, d, 0], partner
        )

    def gather_pass(t, d):
        for e in range(1, chips):
            gather_chip[t, d, e].wait_recv()
            part = values.at[t, d, :, share_rows(chip_at[chips - e], core), :]
            gather_core[t, d, e] = remote(
                part, part, agc_send.at[t, d, e], agc_recv.at[t, d, e], partner
            )

    def apply(t, d):
        for e in range(chips):
            gather_core[t, d, e].wait_recv()
        if t == 0 and d > 0:
            left_in[d].wait_recv()
        left = left_ops if d == 0 else left_recv[d - 1]

        def one(k, carry):
            block = recv_block[d * slots + k]
            right_matrix = right_ops[block_right[block]]
            left_matrix = left[block_left[block]]
            middle = lax.dot_general(
                values[t, d, k],
                right_matrix,
                (((1,), (1,)), ((), ())),
                preferred_element_type=jnp.float32,
            ).astype(jnp.bfloat16)
            partial[t, d, k] = jnp.dot(
                left_matrix, middle, preferred_element_type=jnp.float32
            ).astype(jnp.bfloat16)
            return carry

        lax.fori_loop(0, slots, one, 0, unroll=True)
        for e in range(chips):
            reduce_core[t, d, e] = remote(
                partial.at[t, d, :, share_rows(chip_at[e], 1 - core), :],
                from_core.at[t, d, e],
                rsc_send.at[t, d, e],
                rsc_recv.at[t, d, e],
                partner,
            )

    def chip_sum(t, d, e, k):
        mine = partial[t, d, k, share_rows(chip_at[e], core), :].astype(jnp.float32)
        return mine + from_core[t, d, e, k].astype(jnp.float32)

    def reduce_pass(t, d):
        for e in range(chips):
            reduce_core[t, d, e].wait_recv()
        for e in range(1, chips):

            def one(k, carry):
                to_chip[t, d, e, k] = chip_sum(t, d, e, k).astype(jnp.bfloat16)
                return carry

            lax.fori_loop(0, slots, one, 0, unroll=True)
            reduce_chip[t, d, e] = remote(
                to_chip.at[t, d, e],
                from_chip.at[t, d, e],
                rsx_send.at[t, d, e],
                rsx_recv.at[t, d, e],
                chip_peer[e],
            )

    def finish(t, d):
        for e in range(1, chips):
            reduce_chip[t, d, e].wait_recv()

        def one(k, carry):
            total = chip_sum(t, d, 0, k)
            for e in range(1, chips):
                total = total + from_chip[t, d, e, k].astype(jnp.float32)
            block = recv_block[d * slots + k]
            row_limit = left_dims[sec_after[d] * left_per + block_left[block]]
            col_limit = right_dims[me * right_per + block_right[block]]
            live = (row_ids < row_limit) & (col_ids < col_limit)
            total = jnp.where(live, total, 0.0).astype(jnp.bfloat16)
            if t == 0:
                values[1, d, k, own_rows, :] = total
            if d == 0:
                returned[t][0, k] = total
            elif t == 1:
                final[d, k] = total
            return carry

        lax.fori_loop(0, slots, one, 0, unroll=True)
        if t == 0:
            gather_start(1, d)
        if d > 0:
            place = senders - d
            back[t, d] = remote(
                values.at[1, d, :, own_rows, :] if t == 0 else final.at[d],
                returned[t].at[place],
                z_send.at[2 + t, d],
                z_recv.at[2 + t, place],
                {"sec": sec_after[d]},
            )

    def give(t, d):
        for e in range(1, senders):
            back[t, e].wait_recv()
        out = (out_first, out_second)[t]

        def one(b, carry):
            place = send_place[b]
            out[b] = returned[t][place // slots, place % slots]
            return carry

        lax.fori_loop(0, blocks, one, 0)

    steps = []
    for d in range(senders):
        chain = [(gather_start, 0)]
        for t in (0, 1):
            chain += [(gather_pass, t), (apply, t), (reduce_pass, t), (finish, t)]
        steps += [(SKEW * d + i, d, f, t) for i, (f, t) in enumerate(chain)]
    for _, d, f, t in sorted(steps, key=lambda s: (s[0], s[1])):
        f(t, d)
    give(0, 0)
    give(1, 0)
    for copy in sent:
        copy.wait_send()


def fused_body(
    psi, left_ops, right_ops, left_dims, right_dims, block_left, block_right, right_owner
):
    senders = lax.axis_size("sec")
    holders = lax.axis_size("op")
    me = lax.axis_index("sec")
    blocks, rows, cols = psi.shape
    slots = -(-blocks // senders)
    share = rows // holders
    chips = holders // CORES
    left_per = left_ops.shape[1]

    owner = right_owner.reshape(senders, blocks)
    ids = jnp.arange(blocks, dtype=jnp.int32)
    same = (owner[:, :, None] == owner[:, None, :]) & (ids[None, None, :] < ids[None, :, None])
    rank = jnp.sum(same.astype(jnp.int32), axis=2)
    offsets = jnp.arange(senders, dtype=jnp.int32)
    slot_ids = jnp.arange(slots, dtype=jnp.int32)
    mine_owner = lax.dynamic_index_in_dim(owner, me, 0, keepdims=False)
    mine_rank = lax.dynamic_index_in_dim(rank, me, 0, keepdims=False)
    send_to = (me - offsets + senders) % senders
    send_pick = (mine_owner[None, None, :] == send_to[:, None, None]) & (
        mine_rank[None, None, :] == slot_ids[None, :, None]
    )
    send_block = jnp.sum(jnp.where(send_pick, ids[None, None, :], 0), axis=2).reshape(-1)
    sender_ids = offsets[:, None]
    global_ids = sender_ids * blocks + ids[None, :]
    from_sec = (me + offsets) % senders
    recv_pick = (
        (owner == me)[None, None]
        & (rank[None, None] == slot_ids[None, :, None, None])
        & (sender_ids[None, None] == from_sec[:, None, None, None])
    )
    recv_block = jnp.sum(jnp.where(recv_pick, global_ids[None, None], 0), axis=(2, 3)).reshape(-1)
    send_place = ((mine_owner - me + senders) % senders) * slots + mine_rank

    smem = pl.BlockSpec(memory_space=pltpu.SMEM)
    vmem = pl.BlockSpec(memory_space=pltpu.VMEM)
    dma = pltpu.SemaphoreType.DMA
    bf = jnp.bfloat16
    result = jax.ShapeDtypeStruct((blocks, share, cols), bf)
    parts = (2, senders, chips, slots, share, cols)
    grid = (2, senders, chips)
    return pl.pallas_call(
        functools.partial(kernel, senders, holders),
        out_shape=(result, result),
        in_specs=[smem] * 7 + [vmem] * 3,
        out_specs=(vmem, vmem),
        scratch_shapes=[
            pltpu.VMEM((senders, slots, share, cols), bf),
            pltpu.VMEM((2, senders, slots, rows, cols), bf),
            pltpu.VMEM((2, senders, slots, rows, cols), bf),
            pltpu.VMEM(parts, bf),
            pltpu.VMEM(parts, bf),
            pltpu.VMEM(parts, bf),
            pltpu.VMEM((senders, slots, share, cols), bf),
            pltpu.VMEM((senders, slots, share, cols), bf),
            pltpu.VMEM((senders, slots, share, cols), bf),
            dma((4, senders)),
            dma((4, senders)),
        ]
        + [dma(grid)] * 8
        + [pltpu.VMEM(left_ops.shape[1:], bf)] * (senders - 1),
        compiler_params=pltpu.CompilerParams(
            collective_id=0, has_side_effects=True, vmem_limit_bytes=VMEM_BUDGET
        ),
        cost_estimate=pl.CostEstimate(
            flops=4 * blocks * rows * cols * (rows + cols),
            bytes_accessed=8 * blocks * rows * cols,
            transcendentals=0,
        ),
    )(
        send_block,
        recv_block,
        send_place,
        left_dims,
        right_dims,
        block_left,
        block_right,
        psi,
        left_ops[0],
        right_ops[0],
    )


def any_body(psi, left_ops, right_ops, *tables):
    senders = lax.axis_size("sec")
    whole = 2 * (6 * psi.size + senders * left_ops.size + right_ops.size)
    if whole * 5 // 4 < VMEM_BUDGET and lax.axis_size("op") % CORES == 0:
        return fused_body(psi, left_ops, right_ops, *tables)
    return body(psi, left_ops, right_ops, *tables)


def solution(mesh):
    return jax.shard_map(
        any_body,
        mesh=mesh,
        in_specs=(
            P(("groups", "sec"), None, None),
            P("op", ("groups", "sec"), None, None),
            P("op", ("groups", "sec"), None, None),
            P("groups"),
            P("groups"),
            P("groups"),
            P("groups"),
            P("groups"),
        ),
        out_specs=(P(("groups", "sec"), "op", None), P(("groups", "sec"), "op", None)),
        check_vma=False,
    )
```

```python
import functools

import jax
import jax.numpy as jnp
from jax import lax
from jax.experimental import pallas as pl
from jax.experimental.pallas import tpu as pltpu
from jax.sharding import PartitionSpec as P


def block_masks(row_count, col_count, left_dim, right_dim):
    row_ids = lax.broadcasted_iota(jnp.int32, (1, row_count, 1), 1)
    col_ids = lax.broadcasted_iota(jnp.int32, (1, 1, col_count), 2)
    return (row_ids < left_dim[:, None, None]) & (col_ids < right_dim[:, None, None])


def left_apply(matrices, values):
    return jnp.einsum("pra,pac->prc", matrices, values, preferred_element_type=jnp.float32).astype(
        jnp.bfloat16
    )


def right_apply(matrices, values):
    return jnp.einsum("prc,pdc->prd", values, matrices, preferred_element_type=jnp.float32).astype(
        jnp.bfloat16
    )


def op_combine(terms, live_mask, row_share, op_index):
    own_rows = lax.psum_scatter(
        terms.astype(jnp.bfloat16), "op", scatter_dimension=1, tiled=True
    ).astype(jnp.float32)
    own_mask = lax.dynamic_slice_in_dim(live_mask, op_index * row_share, row_share, 1)
    own_rows = jnp.where(own_mask, own_rows, 0.0).astype(jnp.bfloat16)
    full_sigma = lax.all_gather(own_rows, "op", axis=1, tiled=True)
    return (full_sigma, own_rows)


def body(psi, left_ops, right_ops, left_dims, right_dims, block_left, block_right, right_owner):
    senders = lax.axis_size("sec")
    holders = lax.axis_size("op")
    my_index = lax.axis_index("sec")
    op_index = lax.axis_index("op")
    block_count, left_rows, right_cols = psi.shape
    peer_slots = -(-block_count // senders)
    buffer_len = senders * peer_slots
    left_per = left_ops.shape[1]
    right_per = right_ops.shape[1]
    row_share = left_rows // holders
    owner_table = right_owner.reshape(senders, block_count)
    same_owner = owner_table[:, :, None] == owner_table[:, None, :]
    earlier = lax.broadcasted_iota(jnp.int32, (block_count, block_count), 1) < lax.broadcasted_iota(
        jnp.int32, (block_count, block_count), 0
    )
    order_rank = jnp.sum((same_owner & earlier[None]).astype(jnp.int32), axis=2)
    sender_ids = lax.broadcasted_iota(jnp.int32, (senders, block_count), 0)
    mine_owner = lax.dynamic_index_in_dim(owner_table, my_index, 0, keepdims=False)
    mine_rank = lax.dynamic_index_in_dim(order_rank, my_index, 0, keepdims=False)
    send_pos = mine_owner * peer_slots + mine_rank
    mine_left = lax.dynamic_slice_in_dim(block_left, my_index * block_count, block_count)
    mine_right = lax.dynamic_slice_in_dim(block_right, my_index * block_count, block_count)
    left_mask = block_masks(
        left_rows,
        right_cols,
        left_dims[my_index * left_per + mine_left],
        right_dims[mine_owner * right_per + mine_right],
    )
    slot_ids = jnp.arange(buffer_len, dtype=jnp.int32)
    recv_pos = (sender_ids * peer_slots + order_rank).reshape(-1)
    recv_select = (right_owner == my_index)[None, :] & (recv_pos[None, :] == slot_ids[:, None])
    recv_right = jnp.sum(jnp.where(recv_select, block_right[None, :], 0), axis=1)
    right_matrices = right_ops[0][recv_right]
    left_matrices = left_ops[0][mine_left]
    inputs = jnp.where(left_mask, psi, jnp.zeros_like(psi))
    first_terms = left_apply(left_matrices, inputs)
    operators_back = lax.all_to_all(right_matrices, "sec", split_axis=0, concat_axis=0, tiled=True)
    mine_matrices = jnp.take(operators_back, send_pos, axis=0)
    partial_terms = right_apply(mine_matrices, first_terms)
    full_sigma, sigma_first = op_combine(
        partial_terms.astype(jnp.float32), left_mask, row_share, op_index
    )
    second_terms = left_apply(left_matrices, right_apply(mine_matrices, full_sigma))
    final_rows = lax.psum_scatter(
        second_terms.astype(jnp.float32).astype(jnp.bfloat16), "op", scatter_dimension=1, tiled=True
    ).astype(jnp.float32)
    final_mask = lax.dynamic_slice_in_dim(left_mask, op_index * row_share, row_share, 1)
    sigma_second = jnp.where(final_mask, final_rows, 0.0).astype(jnp.bfloat16)
    return (sigma_first, sigma_second)


MESH = pl.DeviceIdType.MESH
CORES = 2
VMEM_BUDGET = 40 * 2**20


def pair(a, b, count):
    out, bit = 0, 1
    while bit < count:
        out = out + (a // bit + b // bit) % 2 * bit
        bit *= 2
    return out


def kernel(
    senders,
    holders,
    send_block,
    recv_block,
    send_place,
    left_dims_hbm,
    right_dims_hbm,
    block_left_hbm,
    block_right_hbm,
    psi_hbm,
    left_hbm,
    right_hbm,
    out_first,
    out_second,
    left_dims,
    right_dims,
    block_left,
    block_right,
    psi,
    left_ops,
    right_ops,
    fetch_sem,
    packed,
    values,
    partial,
    from_core,
    to_chip,
    from_chip,
    final,
    returned_first,
    returned_second,
    z_send,
    z_recv,
    agx_send,
    agx_recv,
    agc_send,
    agc_recv,
    rsc_send,
    rsc_recv,
    rsx_send,
    rsx_recv,
    *left_recv,
):
    me = lax.axis_index("sec")
    op = lax.axis_index("op")
    chips = holders // CORES
    chip, core = op // CORES, op % CORES
    blocks, rows, cols = psi_hbm.shape
    left_per, right_per = left_ops.shape[0], right_ops.shape[0]
    slots = values.shape[2]
    share = rows // holders
    returned = (returned_first, returned_second)

    def share_rows(chip_index, core_index):
        start = (chip_index * CORES + core_index) * share
        return pl.ds(pl.multiple_of(start, share), share)

    own_rows = share_rows(chip, core)
    partner = {"op": chip * CORES + (1 - core)}
    chip_at = [lax.rem(chip + e, chips) for e in range(chips)]
    chip_peer = [{"op": c * CORES + core} for c in chip_at]
    sec_at = [pair(me, d, senders) for d in range(senders)]

    fetches = [
        pltpu.make_async_copy(src, dst, fetch_sem.at[i])
        for i, (src, dst) in enumerate(
            (
                (psi_hbm.at[:, own_rows, :], psi),
                (left_dims_hbm, left_dims),
                (right_dims_hbm, right_dims),
                (block_left_hbm, block_left),
                (block_right_hbm, block_right),
                (left_hbm, left_ops),
                (right_hbm, right_ops),
            )
        )
    ]
    for fetch in fetches:
        fetch.start()

    barrier = pltpu.get_barrier_semaphore()
    peers = [{"sec": sec_at[d]} for d in range(1, senders)] + [partner] + chip_peer[1:]
    for peer in peers:
        pl.semaphore_signal(barrier, inc=1, device_id=peer, device_id_type=MESH)

    row_ids = lax.broadcasted_iota(jnp.int32, (share, cols), 0) + op * share
    col_ids = lax.broadcasted_iota(jnp.int32, (share, cols), 1)

    def pack(d):
        def one(k, carry):
            block = send_block[d * slots + k]
            value = psi[block].astype(jnp.float32)
            gb = me * blocks + block
            row_limit = left_dims[me * left_per + block_left[gb]]
            col_limit = right_dims[sec_at[d] * right_per + block_right[gb]]
            live = (row_ids < row_limit) & (col_ids < col_limit)
            value = jnp.where(live, value, 0.0).astype(jnp.bfloat16)
            if d == 0:
                values[0, 0, k, own_rows, :] = value
            else:
                packed[d, k] = value
            return carry

        lax.fori_loop(0, slots, one, 0, unroll=True)

    def remote(src, dst, send_sem, recv_sem, device):
        copy = pltpu.make_async_remote_copy(
            src_ref=src,
            dst_ref=dst,
            send_sem=send_sem,
            recv_sem=recv_sem,
            device_id=device,
            device_id_type=MESH,
        )
        copy.start()
        sent.append(copy)
        return copy

    sent = []
    inbound, left_in, gather_chip, gather_core, reduce_core, reduce_chip, back = (
        {},
        {},
        {},
        {},
        {},
        {},
        {},
    )

    def send_left(d):
        if 0 < d < senders:
            left_in[d] = remote(
                left_hbm,
                left_recv[d - 1],
                z_send.at[1, d],
                z_recv.at[1, d],
                {"sec": sec_at[d]},
            )

    for fetch in fetches[:5]:
        fetch.wait()
    for d in range(1, senders):
        pack(d)
    pl.semaphore_wait(barrier, len(peers))
    for d in range(1, senders):
        inbound[d] = remote(
            packed.at[d],
            values.at[0, d, :, own_rows, :],
            z_send.at[0, d],
            z_recv.at[0, d],
            {"sec": sec_at[d]},
        )
        if d == 1:
            send_left(1)
    pack(0)

    def gather_start(t, d):
        if t == 0 and d > 0:
            inbound[d].wait_recv()
        if t == 0 and d == 2:
            send_left(2)
        part = values.at[t, d, :, own_rows, :]
        for e in range(1, chips):
            gather_chip[t, d, e] = remote(
                part, part, agx_send.at[t, d, e], agx_recv.at[t, d, e], chip_peer[e]
            )
        gather_core[t, d, 0] = remote(
            part, part, agc_send.at[t, d, 0], agc_recv.at[t, d, 0], partner
        )

    def gather_pass(t, d):
        for e in range(1, chips):
            gather_chip[t, d, e].wait_recv()
            part = values.at[t, d, :, share_rows(chip_at[chips - e], core), :]
            gather_core[t, d, e] = remote(
                part, part, agc_send.at[t, d, e], agc_recv.at[t, d, e], partner
            )

    def apply(t, d):
        for e in range(chips):
            gather_core[t, d, e].wait_recv()
        if t == 0 and d == 0:
            fetches[5].wait()
            fetches[6].wait()
        if t == 0 and d > 0:
            left_in[d].wait_recv()
            if d + 2 > 2:
                send_left(d + 2)
        left = left_ops if d == 0 else left_recv[d - 1]

        def one(k, carry):
            block = recv_block[d * slots + k]
            right_matrix = right_ops[block_right[block]]
            left_matrix = left[block_left[block]]
            middle = lax.dot_general(
                values[t, d, k],
                right_matrix,
                (((1,), (1,)), ((), ())),
                preferred_element_type=jnp.float32,
            ).astype(jnp.bfloat16)
            partial[t, d, k] = jnp.dot(
                left_matrix, middle, preferred_element_type=jnp.float32
            ).astype(jnp.bfloat16)
            return carry

        lax.fori_loop(0, slots, one, 0, unroll=True)
        for e in range(chips):
            reduce_core[t, d, e] = remote(
                partial.at[t, d, :, share_rows(chip_at[e], 1 - core), :],
                from_core.at[t, d, e],
                rsc_send.at[t, d, e],
                rsc_recv.at[t, d, e],
                partner,
            )

    def chip_sum(t, d, e, k):
        mine = partial[t, d, k, share_rows(chip_at[e], core), :].astype(jnp.float32)
        return mine + from_core[t, d, e, k].astype(jnp.float32)

    def reduce_pass(t, d):
        for e in range(chips):
            reduce_core[t, d, e].wait_recv()
        for e in range(1, chips):

            def one(k, carry):
                to_chip[t, d, e, k] = chip_sum(t, d, e, k).astype(jnp.bfloat16)
                return carry

            lax.fori_loop(0, slots, one, 0, unroll=True)
            reduce_chip[t, d, e] = remote(
                to_chip.at[t, d, e],
                from_chip.at[t, d, e],
                rsx_send.at[t, d, e],
                rsx_recv.at[t, d, e],
                chip_peer[e],
            )

    def finish(t, d):
        for e in range(1, chips):
            reduce_chip[t, d, e].wait_recv()

        def one(k, carry):
            total = chip_sum(t, d, 0, k)
            for e in range(1, chips):
                total = total + from_chip[t, d, e, k].astype(jnp.float32)
            block = recv_block[d * slots + k]
            row_limit = left_dims[sec_at[d] * left_per + block_left[block]]
            col_limit = right_dims[me * right_per + block_right[block]]
            live = (row_ids < row_limit) & (col_ids < col_limit)
            total = jnp.where(live, total, 0.0).astype(jnp.bfloat16)
            if t == 0:
                values[1, d, k, own_rows, :] = total
            if d == 0:
                returned[t][0, k] = total
            elif t == 1:
                final[d, k] = total
            return carry

        lax.fori_loop(0, slots, one, 0, unroll=True)
        if t == 0:
            gather_start(1, d)
        if d > 0:
            place = d
            back[t, d] = remote(
                values.at[1, d, :, own_rows, :] if t == 0 else final.at[d],
                returned[t].at[place],
                z_send.at[2 + t, d],
                z_recv.at[2 + t, place],
                {"sec": sec_at[d]},
            )

    def give(t, d):
        for e in range(1, senders):
            back[t, e].wait_recv()
        out = (out_first, out_second)[t]

        def one(b, carry):
            place = send_place[b]
            out[b] = returned[t][place // slots, place % slots]
            return carry

        lax.fori_loop(0, blocks, one, 0)

    steps = []
    for d in range(senders):
        steps += [(d, d, gather_start, 0), (d + 1.5, d, gather_pass, 0)]
        at = 2 + 3 * d
        for t in (0, 1):
            if t == 1:
                steps.append((at + 6, d, gather_pass, 1))
            start = at + 8 * t
            steps += [(start + 2 * i, d, f, t) for i, f in enumerate((apply, reduce_pass, finish))]
    for _, d, f, t in sorted(steps, key=lambda s: (s[0], s[1])):
        f(t, d)
    give(0, 0)
    give(1, 0)
    for copy in sent:
        copy.wait_send()


def fused_body(
    psi, left_ops, right_ops, left_dims, right_dims, block_left, block_right, right_owner
):
    senders = lax.axis_size("sec")
    holders = lax.axis_size("op")
    me = lax.axis_index("sec")
    blocks, rows, cols = psi.shape
    slots = -(-blocks // senders)
    share = rows // holders
    chips = holders // CORES
    left_per = left_ops.shape[1]

    owner = right_owner.reshape(senders, blocks)
    ids = jnp.arange(blocks, dtype=jnp.int32)
    same = (owner[:, :, None] == owner[:, None, :]) & (ids[None, None, :] < ids[None, :, None])
    rank = jnp.sum(same.astype(jnp.int32), axis=2)
    offsets = jnp.arange(senders, dtype=jnp.int32)
    slot_ids = jnp.arange(slots, dtype=jnp.int32)
    mine_owner = lax.dynamic_index_in_dim(owner, me, 0, keepdims=False)
    mine_rank = lax.dynamic_index_in_dim(rank, me, 0, keepdims=False)
    send_to = pair(me, offsets, senders)
    send_pick = (mine_owner[None, None, :] == send_to[:, None, None]) & (
        mine_rank[None, None, :] == slot_ids[None, :, None]
    )
    send_block = jnp.sum(jnp.where(send_pick, ids[None, None, :], 0), axis=2).reshape(-1)
    sender_ids = offsets[:, None]
    global_ids = sender_ids * blocks + ids[None, :]
    from_sec = send_to
    recv_pick = (
        (owner == me)[None, None]
        & (rank[None, None] == slot_ids[None, :, None, None])
        & (sender_ids[None, None] == from_sec[:, None, None, None])
    )
    recv_block = jnp.sum(jnp.where(recv_pick, global_ids[None, None], 0), axis=(2, 3)).reshape(-1)
    send_place = pair(me, mine_owner, senders) * slots + mine_rank

    smem = pl.BlockSpec(memory_space=pltpu.SMEM)
    vmem = pl.BlockSpec(memory_space=pltpu.VMEM)
    hbm = pl.BlockSpec(memory_space=pl.ANY)
    dma = pltpu.SemaphoreType.DMA
    bf = jnp.bfloat16
    result = jax.ShapeDtypeStruct((blocks, share, cols), bf)
    parts = (2, senders, chips, slots, share, cols)
    grid = (2, senders, chips)
    return pl.pallas_call(
        functools.partial(kernel, senders, holders),
        out_shape=(result, result),
        in_specs=[smem] * 3 + [hbm] * 7,
        out_specs=(vmem, vmem),
        scratch_shapes=[
            pltpu.SMEM(left_dims.shape, jnp.int32),
            pltpu.SMEM(right_dims.shape, jnp.int32),
            pltpu.SMEM(block_left.shape, jnp.int32),
            pltpu.SMEM(block_right.shape, jnp.int32),
            pltpu.VMEM((blocks, share, cols), bf),
            pltpu.VMEM(left_ops.shape[1:], bf),
            pltpu.VMEM(right_ops.shape[1:], bf),
            dma((7,)),
            pltpu.VMEM((senders, slots, share, cols), bf),
            pltpu.VMEM((2, senders, slots, rows, cols), bf),
            pltpu.VMEM((2, senders, slots, rows, cols), bf),
            pltpu.VMEM(parts, bf),
            pltpu.VMEM(parts, bf),
            pltpu.VMEM(parts, bf),
            pltpu.VMEM((senders, slots, share, cols), bf),
            pltpu.VMEM((senders, slots, share, cols), bf),
            pltpu.VMEM((senders, slots, share, cols), bf),
            dma((4, senders)),
            dma((4, senders)),
        ]
        + [dma(grid)] * 8
        + [pltpu.VMEM(left_ops.shape[1:], bf)] * (senders - 1),
        compiler_params=pltpu.CompilerParams(
            collective_id=0, has_side_effects=True, vmem_limit_bytes=VMEM_BUDGET
        ),
        cost_estimate=pl.CostEstimate(
            flops=4 * blocks * rows * cols * (rows + cols),
            bytes_accessed=8 * blocks * rows * cols,
            transcendentals=0,
        ),
    )(
        send_block,
        recv_block,
        send_place,
        left_dims,
        right_dims,
        block_left,
        block_right,
        psi,
        left_ops[0],
        right_ops[0],
    )


def any_body(psi, left_ops, right_ops, *tables):
    senders = lax.axis_size("sec")
    whole = 2 * (6 * psi.size + senders * left_ops.size + right_ops.size)
    if whole * 5 // 4 < VMEM_BUDGET and lax.axis_size("op") % CORES == 0 and senders & (senders - 1) == 0:
        return fused_body(psi, left_ops, right_ops, *tables)
    return body(psi, left_ops, right_ops, *tables)


def solution(mesh):
    return jax.shard_map(
        any_body,
        mesh=mesh,
        in_specs=(
            P(("groups", "sec"), None, None),
            P("op", ("groups", "sec"), None, None),
            P("op", ("groups", "sec"), None, None),
            P("groups"),
            P("groups"),
            P("groups"),
            P("groups"),
            P("groups"),
        ),
        out_specs=(P(("groups", "sec"), "op", None), P(("groups", "sec"), "op", None)),
        check_vma=False,
    )
```

```python
import functools

import jax
import jax.numpy as jnp
from jax import lax
from jax.experimental import pallas as pl
from jax.experimental.pallas import tpu as pltpu
from jax.sharding import PartitionSpec as P


def block_masks(row_count, col_count, left_dim, right_dim):
    row_ids = lax.broadcasted_iota(jnp.int32, (1, row_count, 1), 1)
    col_ids = lax.broadcasted_iota(jnp.int32, (1, 1, col_count), 2)
    return (row_ids < left_dim[:, None, None]) & (col_ids < right_dim[:, None, None])


def left_apply(matrices, values):
    return jnp.einsum("pra,pac->prc", matrices, values, preferred_element_type=jnp.float32).astype(
        jnp.bfloat16
    )


def right_apply(matrices, values):
    return jnp.einsum("prc,pdc->prd", values, matrices, preferred_element_type=jnp.float32).astype(
        jnp.bfloat16
    )


def op_combine(terms, live_mask, row_share, op_index):
    own_rows = lax.psum_scatter(
        terms.astype(jnp.bfloat16), "op", scatter_dimension=1, tiled=True
    ).astype(jnp.float32)
    own_mask = lax.dynamic_slice_in_dim(live_mask, op_index * row_share, row_share, 1)
    own_rows = jnp.where(own_mask, own_rows, 0.0).astype(jnp.bfloat16)
    full_sigma = lax.all_gather(own_rows, "op", axis=1, tiled=True)
    return (full_sigma, own_rows)


def body(psi, left_ops, right_ops, left_dims, right_dims, block_left, block_right, right_owner):
    senders = lax.axis_size("sec")
    holders = lax.axis_size("op")
    my_index = lax.axis_index("sec")
    op_index = lax.axis_index("op")
    block_count, left_rows, right_cols = psi.shape
    peer_slots = -(-block_count // senders)
    buffer_len = senders * peer_slots
    left_per = left_ops.shape[1]
    right_per = right_ops.shape[1]
    row_share = left_rows // holders
    owner_table = right_owner.reshape(senders, block_count)
    same_owner = owner_table[:, :, None] == owner_table[:, None, :]
    earlier = lax.broadcasted_iota(jnp.int32, (block_count, block_count), 1) < lax.broadcasted_iota(
        jnp.int32, (block_count, block_count), 0
    )
    order_rank = jnp.sum((same_owner & earlier[None]).astype(jnp.int32), axis=2)
    sender_ids = lax.broadcasted_iota(jnp.int32, (senders, block_count), 0)
    mine_owner = lax.dynamic_index_in_dim(owner_table, my_index, 0, keepdims=False)
    mine_rank = lax.dynamic_index_in_dim(order_rank, my_index, 0, keepdims=False)
    send_pos = mine_owner * peer_slots + mine_rank
    mine_left = lax.dynamic_slice_in_dim(block_left, my_index * block_count, block_count)
    mine_right = lax.dynamic_slice_in_dim(block_right, my_index * block_count, block_count)
    left_mask = block_masks(
        left_rows,
        right_cols,
        left_dims[my_index * left_per + mine_left],
        right_dims[mine_owner * right_per + mine_right],
    )
    slot_ids = jnp.arange(buffer_len, dtype=jnp.int32)
    recv_pos = (sender_ids * peer_slots + order_rank).reshape(-1)
    recv_select = (right_owner == my_index)[None, :] & (recv_pos[None, :] == slot_ids[:, None])
    recv_right = jnp.sum(jnp.where(recv_select, block_right[None, :], 0), axis=1)
    right_matrices = right_ops[0][recv_right]
    left_matrices = left_ops[0][mine_left]
    inputs = jnp.where(left_mask, psi, jnp.zeros_like(psi))
    first_terms = left_apply(left_matrices, inputs)
    operators_back = lax.all_to_all(right_matrices, "sec", split_axis=0, concat_axis=0, tiled=True)
    mine_matrices = jnp.take(operators_back, send_pos, axis=0)
    partial_terms = right_apply(mine_matrices, first_terms)
    full_sigma, sigma_first = op_combine(
        partial_terms.astype(jnp.float32), left_mask, row_share, op_index
    )
    second_terms = left_apply(left_matrices, right_apply(mine_matrices, full_sigma))
    final_rows = lax.psum_scatter(
        second_terms.astype(jnp.float32).astype(jnp.bfloat16), "op", scatter_dimension=1, tiled=True
    ).astype(jnp.float32)
    final_mask = lax.dynamic_slice_in_dim(left_mask, op_index * row_share, row_share, 1)
    sigma_second = jnp.where(final_mask, final_rows, 0.0).astype(jnp.bfloat16)
    return (sigma_first, sigma_second)


MESH = pl.DeviceIdType.MESH
CORES = 2
VMEM_BUDGET = 40 * 2**20
VMEM_LIMIT = 62 * 2**20


def pair(a, b, count):
    out, bit = 0, 1
    while bit < count:
        out = out + (a // bit + b // bit) % 2 * bit
        bit *= 2
    return out


def kernel(
    senders,
    holders,
    send_block,
    recv_block,
    send_place,
    left_dims_hbm,
    right_dims_hbm,
    block_left_hbm,
    block_right_hbm,
    psi_hbm,
    left_hbm,
    right_hbm,
    out_first,
    out_second,
    left_dims,
    right_dims,
    block_left,
    block_right,
    psi,
    left_ops,
    right_ops,
    fetch_sem,
    packed,
    values,
    partial,
    from_core,
    to_chip,
    from_chip,
    final,
    returned_first,
    returned_second,
    z_send,
    z_recv,
    agx_send,
    agx_recv,
    agc_send,
    agc_recv,
    rsc_send,
    rsc_recv,
    rsx_send,
    rsx_recv,
    *left_recv,
):
    me = lax.axis_index("sec")
    op = lax.axis_index("op")
    chips = holders // CORES
    chip, core = op // CORES, op % CORES
    blocks, rows, cols = psi_hbm.shape
    left_per, right_per = left_ops.shape[0], right_ops.shape[0]
    slots = values.shape[2]
    share = rows // holders
    returned = (returned_first, returned_second)

    def share_rows(chip_index, core_index):
        start = (chip_index * CORES + core_index) * share
        return pl.ds(pl.multiple_of(start, share), share)

    own_rows = share_rows(chip, core)
    partner = {"op": chip * CORES + (1 - core)}
    chip_at = [lax.rem(chip + e, chips) for e in range(chips)]
    chip_peer = [{"op": c * CORES + core} for c in chip_at]
    sec_at = [pair(me, d, senders) for d in range(senders)]

    fetches = [
        pltpu.make_async_copy(src, dst, fetch_sem.at[i])
        for i, (src, dst) in enumerate(
            (
                (psi_hbm.at[:, own_rows, :], psi),
                (left_dims_hbm, left_dims),
                (right_dims_hbm, right_dims),
                (block_left_hbm, block_left),
                (block_right_hbm, block_right),
                (left_hbm, left_ops),
                (right_hbm, right_ops),
            )
        )
    ]
    for fetch in fetches:
        fetch.start()

    barrier = pltpu.get_barrier_semaphore()
    peers = [{"sec": sec_at[d]} for d in range(1, senders)] + [partner] + chip_peer[1:]
    for peer in peers:
        pl.semaphore_signal(barrier, inc=1, device_id=peer, device_id_type=MESH)

    row_ids = lax.broadcasted_iota(jnp.int32, (share, cols), 0) + op * share
    col_ids = lax.broadcasted_iota(jnp.int32, (share, cols), 1)

    def pack(d):
        def one(k, carry):
            block = send_block[d * slots + k]
            value = psi[block].astype(jnp.float32)
            gb = me * blocks + block
            row_limit = left_dims[me * left_per + block_left[gb]]
            col_limit = right_dims[sec_at[d] * right_per + block_right[gb]]
            live = (row_ids < row_limit) & (col_ids < col_limit)
            value = jnp.where(live, value, 0.0).astype(jnp.bfloat16)
            if d == 0:
                values[0, 0, k, own_rows, :] = value
            else:
                packed[d, k] = value
            return carry

        lax.fori_loop(0, slots, one, 0, unroll=True)

    def remote(src, dst, send_sem, recv_sem, device):
        copy = pltpu.make_async_remote_copy(
            src_ref=src,
            dst_ref=dst,
            send_sem=send_sem,
            recv_sem=recv_sem,
            device_id=device,
            device_id_type=MESH,
        )
        copy.start()
        sent.append(copy)
        return copy

    sent = []
    inbound, left_in, gather_chip, gather_core, reduce_core, reduce_chip, back = (
        {},
        {},
        {},
        {},
        {},
        {},
        {},
    )

    def send_left(d):
        if 0 < d < senders:
            left_in[d] = remote(
                left_hbm,
                left_recv[d - 1],
                z_send.at[1, d],
                z_recv.at[1, d],
                {"sec": sec_at[d]},
            )

    for fetch in fetches[:5]:
        fetch.wait()
    for d in range(1, senders):
        pack(d)
    pl.semaphore_wait(barrier, len(peers))
    for d in range(1, senders):
        inbound[d] = remote(
            packed.at[d],
            values.at[0, d, :, own_rows, :],
            z_send.at[0, d],
            z_recv.at[0, d],
            {"sec": sec_at[d]},
        )
        if d == 1:
            send_left(1)
    pack(0)

    def gather_start(t, d):
        if t == 0 and d > 0:
            inbound[d].wait_recv()
        if t == 0 and d == 2:
            send_left(2)
        part = values.at[t, d, :, own_rows, :]
        for e in range(1, chips):
            gather_chip[t, d, e] = remote(
                part, part, agx_send.at[t, d, e], agx_recv.at[t, d, e], chip_peer[e]
            )
        gather_core[t, d, 0] = remote(
            part, part, agc_send.at[t, d, 0], agc_recv.at[t, d, 0], partner
        )

    def gather_pass(t, d):
        for e in range(1, chips):
            gather_chip[t, d, e].wait_recv()
            part = values.at[t, d, :, share_rows(chip_at[chips - e], core), :]
            gather_core[t, d, e] = remote(
                part, part, agc_send.at[t, d, e], agc_recv.at[t, d, e], partner
            )

    def apply(t, d):
        for e in range(chips):
            gather_core[t, d, e].wait_recv()
        if t == 0 and d == 0:
            fetches[5].wait()
            fetches[6].wait()
        if t == 0 and d > 0:
            left_in[d].wait_recv()
            if d + 2 > 2:
                send_left(d + 2)
        left = left_ops if d == 0 else left_recv[d - 1]

        def one(k, carry):
            block = recv_block[d * slots + k]
            right_matrix = right_ops[block_right[block]]
            left_matrix = left[block_left[block]]
            middle = lax.dot_general(
                values[t, d, k],
                right_matrix,
                (((1,), (1,)), ((), ())),
                preferred_element_type=jnp.float32,
            ).astype(jnp.bfloat16)
            partial[t, d, k] = jnp.dot(
                left_matrix, middle, preferred_element_type=jnp.float32
            ).astype(jnp.bfloat16)
            return carry

        lax.fori_loop(0, slots, one, 0, unroll=True)
        for e in range(chips):
            reduce_core[t, d, e] = remote(
                partial.at[t, d, :, share_rows(chip_at[e], 1 - core), :],
                from_core.at[t, d, e],
                rsc_send.at[t, d, e],
                rsc_recv.at[t, d, e],
                partner,
            )

    def chip_sum(t, d, e, k):
        mine = partial[t, d, k, share_rows(chip_at[e], core), :].astype(jnp.float32)
        return mine + from_core[t, d, e, k].astype(jnp.float32)

    def reduce_pass(t, d):
        for e in range(chips):
            reduce_core[t, d, e].wait_recv()
        for e in range(1, chips):

            def one(k, carry):
                to_chip[t, d, e, k] = chip_sum(t, d, e, k).astype(jnp.bfloat16)
                return carry

            lax.fori_loop(0, slots, one, 0, unroll=True)
            reduce_chip[t, d, e] = remote(
                to_chip.at[t, d, e],
                from_chip.at[t, d, e],
                rsx_send.at[t, d, e],
                rsx_recv.at[t, d, e],
                chip_peer[e],
            )

    def finish(t, d):
        for e in range(1, chips):
            reduce_chip[t, d, e].wait_recv()

        def one(k, carry):
            total = chip_sum(t, d, 0, k)
            for e in range(1, chips):
                total = total + from_chip[t, d, e, k].astype(jnp.float32)
            block = recv_block[d * slots + k]
            row_limit = left_dims[sec_at[d] * left_per + block_left[block]]
            col_limit = right_dims[me * right_per + block_right[block]]
            live = (row_ids < row_limit) & (col_ids < col_limit)
            total = jnp.where(live, total, 0.0).astype(jnp.bfloat16)
            if t == 0:
                values[1, d, k, own_rows, :] = total
            if d == 0:
                returned[t][0, k] = total
            elif t == 1:
                final[d, k] = total
            return carry

        lax.fori_loop(0, slots, one, 0, unroll=True)
        if t == 0:
            gather_start(1, d)
        if d > 0:
            place = d
            back[t, d] = remote(
                values.at[1, d, :, own_rows, :] if t == 0 else final.at[d],
                returned[t].at[place],
                z_send.at[2 + t, d],
                z_recv.at[2 + t, place],
                {"sec": sec_at[d]},
            )

    def give(t, d):
        for e in range(1, senders):
            back[t, e].wait_recv()
        out = (out_first, out_second)[t]

        def one(b, carry):
            place = send_place[b]
            out[b] = returned[t][place // slots, place % slots]
            return carry

        lax.fori_loop(0, blocks, one, 0)

    steps = []
    for d in range(senders):
        steps += [(d, d, gather_start, 0), (d + 1.5, d, gather_pass, 0)]
        at = 2 + 3 * d
        for t in (0, 1):
            if t == 1:
                steps.append((at + 6, d, gather_pass, 1))
            start = at + 8 * t
            steps += [(start + 2 * i, d, f, t) for i, f in enumerate((apply, reduce_pass, finish))]
    for _, d, f, t in sorted(steps, key=lambda s: (s[0], s[1])):
        f(t, d)
    give(0, 0)
    give(1, 0)
    for copy in sent:
        copy.wait_send()


def fused_body(
    psi, left_ops, right_ops, left_dims, right_dims, block_left, block_right, right_owner
):
    senders = lax.axis_size("sec")
    holders = lax.axis_size("op")
    me = lax.axis_index("sec")
    blocks, rows, cols = psi.shape
    slots = -(-blocks // senders)
    share = rows // holders
    chips = holders // CORES
    left_per = left_ops.shape[1]

    owner = right_owner.reshape(senders, blocks)
    ids = jnp.arange(blocks, dtype=jnp.int32)
    same = (owner[:, :, None] == owner[:, None, :]) & (ids[None, None, :] < ids[None, :, None])
    rank = jnp.sum(same.astype(jnp.int32), axis=2)
    offsets = jnp.arange(senders, dtype=jnp.int32)
    slot_ids = jnp.arange(slots, dtype=jnp.int32)
    mine_owner = lax.dynamic_index_in_dim(owner, me, 0, keepdims=False)
    mine_rank = lax.dynamic_index_in_dim(rank, me, 0, keepdims=False)
    send_to = pair(me, offsets, senders)
    send_pick = (mine_owner[None, None, :] == send_to[:, None, None]) & (
        mine_rank[None, None, :] == slot_ids[None, :, None]
    )
    send_block = jnp.sum(jnp.where(send_pick, ids[None, None, :], 0), axis=2).reshape(-1)
    sender_ids = offsets[:, None]
    global_ids = sender_ids * blocks + ids[None, :]
    from_sec = send_to
    recv_pick = (
        (owner == me)[None, None]
        & (rank[None, None] == slot_ids[None, :, None, None])
        & (sender_ids[None, None] == from_sec[:, None, None, None])
    )
    recv_block = jnp.sum(jnp.where(recv_pick, global_ids[None, None], 0), axis=(2, 3)).reshape(-1)
    send_place = pair(me, mine_owner, senders) * slots + mine_rank

    smem = pl.BlockSpec(memory_space=pltpu.SMEM)
    vmem = pl.BlockSpec(memory_space=pltpu.VMEM)
    hbm = pl.BlockSpec(memory_space=pl.ANY)
    dma = pltpu.SemaphoreType.DMA
    bf = jnp.bfloat16
    result = jax.ShapeDtypeStruct((blocks, share, cols), bf)
    parts = (2, senders, chips, slots, share, cols)
    grid = (2, senders, chips)
    return pl.pallas_call(
        functools.partial(kernel, senders, holders),
        out_shape=(result, result),
        in_specs=[smem] * 3 + [hbm] * 7,
        out_specs=(vmem, vmem),
        scratch_shapes=[
            pltpu.SMEM(left_dims.shape, jnp.int32),
            pltpu.SMEM(right_dims.shape, jnp.int32),
            pltpu.SMEM(block_left.shape, jnp.int32),
            pltpu.SMEM(block_right.shape, jnp.int32),
            pltpu.VMEM((blocks, share, cols), bf),
            pltpu.VMEM(left_ops.shape[1:], bf),
            pltpu.VMEM(right_ops.shape[1:], bf),
            dma((7,)),
            pltpu.VMEM((senders, slots, share, cols), bf),
            pltpu.VMEM((2, senders, slots, rows, cols), bf),
            pltpu.VMEM((2, senders, slots, rows, cols), bf),
            pltpu.VMEM(parts, bf),
            pltpu.VMEM(parts, bf),
            pltpu.VMEM(parts, bf),
            pltpu.VMEM((senders, slots, share, cols), bf),
            pltpu.VMEM((senders, slots, share, cols), bf),
            pltpu.VMEM((senders, slots, share, cols), bf),
            dma((4, senders)),
            dma((4, senders)),
        ]
        + [dma(grid)] * 8
        + [pltpu.VMEM(left_ops.shape[1:], bf)] * (senders - 1),
        compiler_params=pltpu.CompilerParams(
            collective_id=0, has_side_effects=True, vmem_limit_bytes=VMEM_LIMIT
        ),
        cost_estimate=pl.CostEstimate(
            flops=4 * blocks * rows * cols * (rows + cols),
            bytes_accessed=8 * blocks * rows * cols,
            transcendentals=0,
        ),
    )(
        send_block,
        recv_block,
        send_place,
        left_dims,
        right_dims,
        block_left,
        block_right,
        psi,
        left_ops[0],
        right_ops[0],
    )


def any_body(psi, left_ops, right_ops, *tables):
    senders = lax.axis_size("sec")
    whole = 2 * (6 * psi.size + senders * left_ops.size + right_ops.size)
    if whole * 5 // 4 < VMEM_BUDGET and lax.axis_size("op") % CORES == 0 and senders & (senders - 1) == 0:
        return fused_body(psi, left_ops, right_ops, *tables)
    return body(psi, left_ops, right_ops, *tables)


def solution(mesh):
    return jax.shard_map(
        any_body,
        mesh=mesh,
        in_specs=(
            P(("groups", "sec"), None, None),
            P("op", ("groups", "sec"), None, None),
            P("op", ("groups", "sec"), None, None),
            P("groups"),
            P("groups"),
            P("groups"),
            P("groups"),
            P("groups"),
        ),
        out_specs=(P(("groups", "sec"), "op", None), P(("groups", "sec"), "op", None)),
        check_vma=False,
    )
```
